32 devices in a mesh: front: 8 (over z, y), pair: 4 (over x, core).
Axes of the slice: x: 2, y: 2, z: 4, core: 2. Of those that a mesh axis runs over, the one named last changes fastest.
Arguments:
- pivot_block: float32 [8, 768, 768], P('front', 'pair'), may hold values from -1 to 8, as said below
- coupling_rows: float32 [8, 2304, 768], P('front', 'pair'), may hold values from -0.6 to 0.6
- trailing_block: float32 [8, 2304, 2304], P('front', 'pair'), may hold values from -6 to 6
- index_map: int32 [8, 2304], replicated, may hold values from 0 to 3071, as said below
Outputs:
- panel_factor: float32 [8, 2304, 768], P('front', 'pair')
- parent_front: float32 [3072, 8, 768], P('pair', 'front')
The draws below stay inside these ranges and needn't reach their ends.
Inputs may be any that keep to these rules, and one draw needn't show every extreme that they name: pivot_block[c] is symmetric positive definite. For each child c and row block p, the entries index_map[c, p * 576 + a] for a below 576 are distinct, rising, and lie in p * 768 to (p + 1) * 768 - 1.
All inputs are finite; a program needn't handle non-finite values.
Results may differ from the reference program's by a relative error of at most 0.0029.
Values may be sent and summed in bfloat16 or wider, within the bound.
A program may use at most 128 MiB of HBM per device.

```python
import jax
import jax.numpy as jnp
from jax import lax

PIV = 768
UPD = 2304
PO = 3072
CHILDREN = 8
PARENTS = 2
UPD_BLK = 576
PAR_BLK = 768


def draw_pivot_block(key, part):
    first_key, second_key = jax.random.split(jax.random.fold_in(key, 11))
    normals = jax.random.normal(first_key, (CHILDREN, PIV, PIV), jnp.float32)
    gram = jnp.einsum('cik,cjk->cij', normals, normals) / PIV
    lifted = jax.random.uniform(second_key, (CHILDREN, PIV), jnp.float32, 1.0, 2.0)
    return gram + lifted[:, :, None] * jnp.eye(PIV, dtype=jnp.float32)[None, :, :]


def draw_index_map(key, part):
    blocks = PO // PAR_BLK
    keys = jax.random.split(jax.random.fold_in(key, 7), CHILDREN * blocks)
    picks = jax.vmap(lambda one_key: jnp.sort(jax.random.permutation(one_key, PAR_BLK)[:UPD_BLK]))(keys)
    offsets = jnp.arange(CHILDREN * blocks, dtype=jnp.int32) % blocks * PAR_BLK
    return (picks.astype(jnp.int32) + offsets[:, None]).reshape(CHILDREN, UPD).astype(jnp.int32)


def block_levels(own_key, shape, cuts, smallest, top_value):
    def one(axis_at, shards_of):
        steps = jax.random.uniform(jax.random.fold_in(jax.random.fold_in(own_key, 6), axis_at), (shards_of,), jnp.float32, smallest / len(cuts), top_value / len(cuts))
        return jnp.repeat(jnp.exp(steps), shape[axis_at] // shards_of).reshape((-1,) + (1,) * (len(shape) - axis_at - 1))

    factor_of = one(*cuts[0])
    for cut in cuts[1:]:
        factor_of = factor_of * one(*cut)
    return factor_of


def bell_draw(stream_key, extent, spread, most, cuts=(), kind=jnp.bfloat16):
    result = spread * jax.random.normal(stream_key, extent, jnp.float32)
    if cuts:
        result = result * block_levels(stream_key, extent, cuts, -0.22, 0.18)
    return jnp.clip(result, -most, most).astype(kind)


def setup_inputs(seed: int = 0) -> dict:
    key_list = jax.random.split(jax.random.key(seed), 5)
    return {
        "pivot_block": draw_pivot_block(jax.random.fold_in(key_list[4], 71), 0),
        "coupling_rows": bell_draw(key_list[1], (CHILDREN, UPD, PIV), 0.1, 0.6, ((0, 8), (1, 4)), jnp.float32),
        "trailing_block": bell_draw(key_list[2], (CHILDREN, UPD, UPD), 1.0, 6.0, ((0, 8), (1, 4)), jnp.float32),
        "index_map": draw_index_map(jax.random.fold_in(key_list[4], 71), 0),
    }


def eliminate(pivot, coupling, trailing):
    lower_factor = jnp.linalg.cholesky(pivot)
    factor = jax.scipy.linalg.solve_triangular(lower_factor, coupling.T, lower=True).T
    rounded = lax.optimization_barrier(factor.astype(jnp.bfloat16))
    panel_half = rounded.astype(jnp.float32)
    product = jnp.dot(panel_half, panel_half.T, precision=lax.Precision.HIGHEST)
    return (factor, (trailing - product).astype(jnp.bfloat16))

def assemble(group):
    pivots, couplings, trailings, maps = group
    front_sum = jnp.zeros((PO, PO), jnp.float32)
    factors = []
    for member in range(4):
        factor, update = eliminate(pivots[member], couplings[member], trailings[member])
        rows_map = maps[member].astype(jnp.int32)
        front_sum = front_sum.at[rows_map[:, None], rows_map[None, :]].add(update.astype(jnp.float32))
        factors.append(factor)
    return (jnp.stack(factors), front_sum)

def reference(pivot_block, coupling_rows, trailing_block, index_map):
    groups = (pivot_block.reshape(PARENTS, 4, PIV, PIV), coupling_rows.reshape(PARENTS, 4, UPD, PIV), trailing_block.reshape(PARENTS, 4, UPD, UPD), index_map.reshape(PARENTS, 4, UPD))
    factors, fronts = lax.map(assemble, groups)
    panel_factor = factors.reshape(CHILDREN, UPD, PIV)
    parent_front = fronts.reshape(PARENTS, PO, 4, PO // 4).transpose(1, 0, 2, 3).reshape(PO, 4 * PARENTS, PO // 4)
    return (panel_factor, parent_front)
```

```python
import jax
import jax.numpy as jnp
from jax import lax
from jax.experimental import pallas as pl
from jax.experimental.pallas import tpu as pltpu
from jax.sharding import PartitionSpec as P

PO = 3072
SIBLINGS = 4
BLK = 128
SUB = 8


def dot_t(a, b):
    return lax.dot_general(a, b, (((1,), (1,)), ((), ())), preferred_element_type=jnp.float32)


def halves(value):
    high = value.astype(jnp.bfloat16)
    return high, (value - high.astype(jnp.float32)).astype(jnp.bfloat16)


def dot3(a, b):
    return dot_t(a[0], b[0]) + (dot_t(a[0], b[1]) + dot_t(a[1], b[0]))


def inverse_factor(block):
    size = block.shape[0]
    sub = lax.broadcasted_iota(jnp.int32, (SUB, size), 0)
    lane = lax.broadcasted_iota(jnp.int32, (SUB, size), 1)
    rest = block
    done = []
    for start in range(0, size, SUB):
        rows = size - start
        cols = [
            jnp.broadcast_to(rest[:, start + j : start + j + 1], (rows, size)) for j in range(SUB)
        ]
        rest_lane = lax.broadcasted_iota(jnp.int32, (rows, size), 1)
        rest = jnp.where((rest_lane >= start) & (rest_lane < start + SUB), 0.0, rest)
        slab = jnp.where(lane - start == sub, 1.0, rest[:SUB])
        top = [c[:SUB] for c in cols]
        more = rows > SUB
        if more:
            below = rest[SUB:]
            low = [c[SUB:] for c in cols]
        scale = jnp.ones((SUB, size), jnp.float32)
        for t in range(SUB):
            pivot = top[t][t : t + 1, :]
            recip = 1.0 / pivot
            scale = jnp.where(sub == t, lax.rsqrt(pivot), scale)
            for j in range(t + 1, SUB):
                mult = top[j][t : t + 1, :] * recip
                top[j] = top[j] - top[t] * mult
                if more:
                    low[j] = low[j] - low[t] * mult
            row = slab[t : t + 1, :] * recip
            slab = slab - jnp.where(sub > t, top[t], 0.0) * row
            if more:
                below = below - low[t] * row
        done.append(slab * scale)
        if more:
            rest = below
    whole = jnp.concatenate(done, axis=0)
    row_id = lax.broadcasted_iota(jnp.int32, (size, size), 0)
    col_id = lax.broadcasted_iota(jnp.int32, (size, size), 1)
    return jnp.where(col_id <= row_id, whole, 0.0)


def factor_kernel(pivot_ref, coupling_ref, factor_ref, half_ref, work, rows_left):
    order = pivot_ref.shape[0]
    work[...] = pivot_ref[...]
    rows_left[...] = coupling_ref[...]

    def step(k, carry):
        at = pl.ds(pl.multiple_of(k * BLK, BLK), BLK)
        inverse = halves(inverse_factor(work[at, at]))
        panel = halves(dot3(halves(work[:, at]), inverse))
        solved = dot3(halves(rows_left[:, at]), inverse)
        factor_ref[:, at] = solved
        half_ref[:, at] = solved.astype(jnp.bfloat16)
        solved = halves(solved)
        for c in range(0, order, 256):
            cs = slice(c, c + 256)
            part = (panel[0][cs], panel[1][cs])
            work[:, cs] = work[:, cs] - dot3(panel, part)
            rows_left[:, cs] = rows_left[:, cs] - dot3(solved, part)
        return carry

    lax.fori_loop(0, order // BLK, step, 0)


def factor_rows(pivot, coupling):
    order = pivot.shape[0]
    rows = coupling.shape[0]
    return pl.pallas_call(
        factor_kernel,
        out_shape=(
            jax.ShapeDtypeStruct((rows, order), jnp.float32),
            jax.ShapeDtypeStruct((rows, order), jnp.bfloat16),
        ),
        in_specs=[pl.BlockSpec(memory_space=pltpu.VMEM)] * 2,
        out_specs=[pl.BlockSpec(memory_space=pltpu.VMEM)] * 2,
        scratch_shapes=[
            pltpu.VMEM((order, order), jnp.float32),
            pltpu.VMEM((rows, order), jnp.float32),
        ],
        compiler_params=pltpu.CompilerParams(vmem_limit_bytes=48 * 2**20),
    )(pivot, coupling)


def body(pivot_block, coupling_rows, trailing_block, index_map):
    child_id = lax.axis_index("front")
    pair_id = lax.axis_index("pair")
    pairs = lax.axis_size("pair")
    fronts = lax.axis_size("front")
    whole_pivot = lax.all_gather(pivot_block[0], "pair", axis=0, tiled=True)
    factor, panel_half = factor_rows(whole_pivot, coupling_rows[0])
    whole_half = lax.all_gather(panel_half, "pair", axis=0, tiled=True)
    upd_rows = panel_half.shape[0]
    upd_cols = trailing_block.shape[2] // SIBLINGS
    row_count = PO // pairs
    col_count = PO // SIBLINGS
    sibling = child_id % SIBLINGS

    def piece(block):
        there = lax.dynamic_slice_in_dim(whole_half, block * upd_cols, upd_cols)
        old = lax.dynamic_slice_in_dim(trailing_block[0], block * upd_cols, upd_cols, axis=1)
        return (old - dot_t(panel_half, there)).astype(jnp.bfloat16)

    pieces = []
    for apart in (3, 1, 2):
        mine = piece(sibling ^ apart)
        pieces.append(
            (apart, lax.ppermute(mine, "front", [(i, i ^ apart) for i in range(fronts)]))
        )
    pieces.append((0, piece(sibling)))

    assembled = jnp.zeros((row_count, col_count), jnp.float32)
    for apart, value in pieces:
        child_map = lax.dynamic_index_in_dim(index_map, child_id ^ apart, 0, keepdims=False)
        rows_map = lax.dynamic_slice_in_dim(child_map, pair_id * upd_rows, upd_rows)
        cols_map = lax.dynamic_slice_in_dim(child_map, sibling * upd_cols, upd_cols)
        row_hot = (
            rows_map[None, :] - pair_id * row_count == jnp.arange(row_count, dtype=jnp.int32)[:, None]
        ).astype(jnp.bfloat16)
        col_hot = (
            cols_map[:, None] - sibling * col_count == jnp.arange(col_count, dtype=jnp.int32)[None, :]
        ).astype(jnp.bfloat16)
        moved = jnp.dot(value, col_hot, preferred_element_type=jnp.float32).astype(jnp.bfloat16)
        assembled = assembled + jnp.dot(row_hot, moved, preferred_element_type=jnp.float32)
    return (factor[None, :, :], assembled[:, None, :])


def solution(mesh):
    in_specs = (P("front", "pair", None), P("front", "pair", None), P("front", "pair", None), P())
    out_specs = (P("front", "pair", None), P("pair", "front", None))
    return jax.shard_map(body, mesh=mesh, in_specs=in_specs, out_specs=out_specs, check_vma=False)
```

```python
import jax
import jax.numpy as jnp
from jax import lax
from jax.experimental import pallas as pl
from jax.experimental.pallas import tpu as pltpu
from jax.sharding import PartitionSpec as P

PO = 3072
SIBLINGS = 4
BLK = 128
SUB = 8
MESH = pl.DeviceIdType.MESH


def dot_t(a, b):
    return lax.dot_general(a, b, (((1,), (1,)), ((), ())), preferred_element_type=jnp.float32)


def halves(value):
    high = value.astype(jnp.bfloat16)
    return high, (value - high.astype(jnp.float32)).astype(jnp.bfloat16)


def dot3(a, b):
    return dot_t(a[0], b[0]) + (dot_t(a[0], b[1]) + dot_t(a[1], b[0]))


def inverse_factor(block):
    size = block.shape[0]
    sub = lax.broadcasted_iota(jnp.int32, (SUB, size), 0)
    lane = lax.broadcasted_iota(jnp.int32, (SUB, size), 1)
    rest = block
    done = []
    for start in range(0, size, SUB):
        rows = size - start
        cols = [
            jnp.broadcast_to(rest[:, start + j : start + j + 1], (rows, size)) for j in range(SUB)
        ]
        rest_lane = lax.broadcasted_iota(jnp.int32, (rows, size), 1)
        rest = jnp.where((rest_lane >= start) & (rest_lane < start + SUB), 0.0, rest)
        slab = jnp.where(lane - start == sub, 1.0, rest[:SUB])
        top = [c[:SUB] for c in cols]
        more = rows > SUB
        if more:
            below = rest[SUB:]
            low = [c[SUB:] for c in cols]
        scale = jnp.ones((SUB, size), jnp.float32)
        for t in range(SUB):
            pivot = top[t][t : t + 1, :]
            recip = 1.0 / pivot
            scale = jnp.where(sub == t, lax.rsqrt(pivot), scale)
            for j in range(t + 1, SUB):
                mult = top[j][t : t + 1, :] * recip
                top[j] = top[j] - top[t] * mult
                if more:
                    low[j] = low[j] - low[t] * mult
            row = slab[t : t + 1, :] * recip
            slab = slab - jnp.where(sub > t, top[t], 0.0) * row
            if more:
                below = below - low[t] * row
        done.append(slab * scale)
        if more:
            rest = below
    whole = jnp.concatenate(done, axis=0)
    row_id = lax.broadcasted_iota(jnp.int32, (size, size), 0)
    col_id = lax.broadcasted_iota(jnp.int32, (size, size), 1)
    return jnp.where(col_id <= row_id, whole, 0.0)


def fused_kernel(
    maps_ref, pivot_ref, coupling_ref, trailing_ref, factor_ref, front_ref,
    raw, work, rows_left, panels, old_flat, old, outgoing, incoming,
    old_sem, piv_send, piv_recv, pan_send, pan_recv, upd_send, upd_recv,
):
    order = pivot_ref.shape[1]
    own_rows = pivot_ref.shape[0]
    upd = coupling_ref.shape[0]
    blocks = order // BLK
    child = lax.axis_index("front")
    me = lax.axis_index("pair")
    sibling = lax.rem(child, SIBLINGS)
    sib_hi, sib_lo = lax.div(sibling, 2), lax.rem(sibling, 2)
    chip, core = lax.div(me, 2), lax.rem(me, 2)
    across = (1 - chip) * 2 + core
    mate = chip * 2 + (1 - core)
    mate_across = (1 - chip) * 2 + (1 - core)

    def relative(apart):
        hi = 1 - sib_hi if apart >= 2 else sib_hi
        lo = 1 - sib_lo if apart % 2 else sib_lo
        return hi * 2 + lo

    def sib_child(apart):
        return child - sibling + relative(apart)

    barrier = pltpu.get_barrier_semaphore()
    for peer in (across, mate):
        pl.semaphore_signal(barrier, inc=1, device_id={"pair": peer}, device_id_type=MESH)
    for apart in (1, 2, 3):
        pl.semaphore_signal(
            barrier, inc=1, device_id={"front": sib_child(apart)}, device_id_type=MESH
        )
    load_old = pltpu.make_async_copy(trailing_ref, old_flat, old_sem)
    load_old.start()
    pl.semaphore_wait(barrier, 5)

    def cols(k):
        return pl.ds(pl.multiple_of(k * BLK, BLK), BLK)

    def pivot_rows(owner):
        return pl.ds(pl.multiple_of(owner * own_rows, 8), own_rows)

    def pivot_copy(kind, k, owner, peer):
        spot = raw.at[pivot_rows(owner), cols(k)]
        return pltpu.make_async_remote_copy(
            src_ref=spot if kind == 2 else pivot_ref.at[:, cols(k)],
            dst_ref=spot,
            send_sem=piv_send.at[kind, k],
            recv_sem=piv_recv.at[kind, k],
            device_id={"pair": peer},
            device_id_type=MESH,
        )

    def panel_copy(kind, k, owner, peer):
        spot = panels.at[owner, :, cols(k)]
        return pltpu.make_async_remote_copy(
            src_ref=spot,
            dst_ref=spot,
            send_sem=pan_send.at[kind, k],
            recv_sem=pan_recv.at[kind, k],
            device_id={"pair": peer},
            device_id_type=MESH,
        )

    def relay(copy, k):
        copy(0, k, across, across).wait_recv()
        copy(2, k, across, mate).start()

    for k in range(blocks):
        pivot_copy(0, k, me, across).start()
        pivot_copy(1, k, me, mate).start()

    raw[pivot_rows(me), :] = pivot_ref[...]
    rows_left[...] = coupling_ref[...]
    work[...] = jnp.zeros_like(work)
    load_old.wait()
    for b in range(SIBLINGS):
        old[b] = old_flat[:, b * upd : (b + 1) * upd]
    relay(pivot_copy, 0)

    row_id = lax.broadcasted_iota(jnp.int32, (order, BLK), 0)

    def step(k, carry):
        at = cols(k)
        pivot_copy(1, k, mate, mate).wait_recv()
        pivot_copy(2, k, mate_across, mate).wait_recv()
        inverse = halves(inverse_factor(raw[at, at] + work[at, at]))

        @pl.when(k + 1 < blocks)
        def _():
            relay(pivot_copy, k + 1)

        @pl.when(k > 0)
        def _():
            relay(panel_copy, k - 1)

        solved = dot3(halves(rows_left[:, at]), inverse)
        factor_ref[:, at] = solved
        panels[me, :, at] = solved.astype(jnp.bfloat16)
        panel_copy(0, k, me, across).start()
        panel_copy(1, k, me, mate).start()
        column = jnp.where(row_id >= k * BLK, raw[:, at] + work[:, at], 0.0)
        panel = halves(dot3(halves(column), inverse))
        solved = halves(solved)
        for c in range(0, order, 256):
            cs = slice(c, c + 256)
            part = (panel[0][cs], panel[1][cs])
            work[:, cs] = work[:, cs] - dot3(panel, part)
            rows_left[:, cs] = rows_left[:, cs] - dot3(solved, part)
        return carry

    lax.fori_loop(0, blocks, step, 0)
    relay(panel_copy, blocks - 1)
    for k in range(blocks):
        panel_copy(1, k, mate, mate).wait_recv()
        panel_copy(2, k, mate_across, mate).wait_recv()

    def update_copy(apart):
        return pltpu.make_async_remote_copy(
            src_ref=outgoing.at[apart],
            dst_ref=incoming.at[apart - 1],
            send_sem=upd_send.at[apart],
            recv_sem=upd_recv.at[apart],
            device_id={"front": sib_child(apart)},
            device_id_type=MESH,
        )

    for apart in (3, 1, 2, 0):
        there = relative(apart)
        outgoing[apart] = (old[there] - dot_t(panels[me], panels[there])).astype(jnp.bfloat16)
        if apart:
            update_copy(apart).start()

    row_count, col_count = front_ref.shape
    target_rows = lax.broadcasted_iota(jnp.int32, (row_count, upd), 0)
    target_cols = lax.broadcasted_iota(jnp.int32, (col_count, upd), 0)
    for apart in (0, 1, 2, 3):
        if apart:
            update_copy(apart).wait_recv()
            value = incoming[apart - 1]
        else:
            value = outgoing[0]
        base = sib_child(apart) * SIBLINGS
        rows_map = maps_ref[pl.ds(base + me, 1), :] - me * row_count
        cols_map = maps_ref[pl.ds(base + sibling, 1), :] - sibling * col_count
        row_hot = jnp.where(target_rows == rows_map, 1.0, 0.0).astype(jnp.bfloat16)
        col_hot = jnp.where(target_cols == cols_map, 1.0, 0.0).astype(jnp.bfloat16)
        moved = dot_t(value, col_hot).astype(jnp.bfloat16)
        placed = jnp.dot(row_hot, moved, preferred_element_type=jnp.float32)
        if apart:
            front_ref[...] += placed
        else:
            front_ref[...] = placed

    for k in range(blocks):
        for kind, owner, peer in ((0, me, across), (1, me, mate), (2, across, mate)):
            pivot_copy(kind, k, owner, peer).wait_send()
            panel_copy(kind, k, owner, peer).wait_send()
    for apart in (1, 2, 3):
        update_copy(apart).wait_send()


def body(pivot_block, coupling_rows, trailing_block, index_map):
    pairs = lax.axis_size("pair")
    own_rows, order = pivot_block.shape[1:]
    upd, upd_all = trailing_block.shape[1:]
    blocks = order // BLK
    row_count, col_count = PO // pairs, PO // SIBLINGS
    maps = index_map.reshape(-1, upd)
    vmem = pl.BlockSpec(memory_space=pltpu.VMEM)
    factor, front = pl.pallas_call(
        fused_kernel,
        out_shape=(
            jax.ShapeDtypeStruct((upd, order), jnp.float32),
            jax.ShapeDtypeStruct((row_count, col_count), jnp.float32),
        ),
        in_specs=[vmem, vmem, vmem, pl.BlockSpec(memory_space=pl.ANY)],
        out_specs=[vmem, vmem],
        scratch_shapes=[
            pltpu.VMEM((order, order), jnp.float32),
            pltpu.VMEM((order, order), jnp.float32),
            pltpu.VMEM((upd, order), jnp.float32),
            pltpu.VMEM((pairs, upd, order), jnp.bfloat16),
            pltpu.VMEM((upd, upd_all), jnp.float32),
            pltpu.VMEM((SIBLINGS, upd, upd), jnp.float32),
            pltpu.VMEM((SIBLINGS, upd, upd), jnp.bfloat16),
            pltpu.VMEM((SIBLINGS - 1, upd, upd), jnp.bfloat16),
            pltpu.SemaphoreType.DMA,
            pltpu.SemaphoreType.DMA((3, blocks)),
            pltpu.SemaphoreType.DMA((3, blocks)),
            pltpu.SemaphoreType.DMA((3, blocks)),
            pltpu.SemaphoreType.DMA((3, blocks)),
            pltpu.SemaphoreType.DMA((SIBLINGS,)),
            pltpu.SemaphoreType.DMA((SIBLINGS,)),
        ],
        compiler_params=pltpu.CompilerParams(
            collective_id=0, has_side_effects=True, vmem_limit_bytes=56 * 2**20
        ),
    )(maps, pivot_block[0], coupling_rows[0], trailing_block[0])
    return (factor[None, :, :], front[:, None, :])


def solution(mesh):
    in_specs = (P("front", "pair", None), P("front", "pair", None), P("front", "pair", None), P())
    out_specs = (P("front", "pair", None), P("pair", "front", None))
    return jax.shard_map(body, mesh=mesh, in_specs=in_specs, out_specs=out_specs, check_vma=False)
```

```python
import jax
import jax.numpy as jnp
from jax import lax
from jax.experimental import pallas as pl
from jax.experimental.pallas import tpu as pltpu
from jax.sharding import PartitionSpec as P

PO = 3072
SIBLINGS = 4
BLK = 128
SUB = 8
MESH = pl.DeviceIdType.MESH


def dot_t(a, b):
    return lax.dot_general(a, b, (((1,), (1,)), ((), ())), preferred_element_type=jnp.float32)


def halves(value):
    high = value.astype(jnp.bfloat16)
    return high, (value - high.astype(jnp.float32)).astype(jnp.bfloat16)


def dot3(a, b):
    return dot_t(
        jnp.concatenate([a[0], a[0], a[1]], axis=1), jnp.concatenate([b[0], b[1], b[0]], axis=1)
    )


def inverse_factor(block):
    size = block.shape[0]
    sub = lax.broadcasted_iota(jnp.int32, (SUB, size), 0)
    lane = lax.broadcasted_iota(jnp.int32, (SUB, size), 1)
    rest = block
    done = []
    for start in range(0, size, SUB):
        rows = size - start
        cols = [
            jnp.broadcast_to(rest[:, start + j : start + j + 1], (rows, size)) for j in range(SUB)
        ]
        rest_lane = lax.broadcasted_iota(jnp.int32, (rows, size), 1)
        rest = jnp.where((rest_lane >= start) & (rest_lane < start + SUB), 0.0, rest)
        slab = jnp.where(lane - start == sub, 1.0, rest[:SUB])
        top = [c[:SUB] for c in cols]
        more = rows > SUB
        if more:
            below = rest[SUB:]
            low = [c[SUB:] for c in cols]
        scale = jnp.ones((SUB, size), jnp.float32)
        for t in range(SUB):
            pivot = top[t][t : t + 1, :]
            recip = 1.0 / pivot
            scale = jnp.where(sub == t, lax.rsqrt(pivot), scale)
            for j in range(t + 1, SUB):
                mult = top[j][t : t + 1, :] * recip
                top[j] = top[j] - top[t] * mult
                if more:
                    low[j] = low[j] - low[t] * mult
            row = slab[t : t + 1, :] * recip
            slab = slab - jnp.where(sub > t, top[t], 0.0) * row
            if more:
                below = below - low[t] * row
        done.append(slab * scale)
        if more:
            rest = below
    whole = jnp.concatenate(done, axis=0)
    row_id = lax.broadcasted_iota(jnp.int32, (size, size), 0)
    col_id = lax.broadcasted_iota(jnp.int32, (size, size), 1)
    return jnp.where(col_id <= row_id, whole, 0.0)


def fused_kernel(
    maps_ref, pivot_ref, coupling_ref, trailing_ref, factor_ref, front_ref,
    raw, work, rows_left, panels, pend, pend_own, old_flat, old,
    outgoing, outgoing_tail, incoming, incoming_tail,
    old_sem, piv_send, piv_recv, pan_send, pan_recv, upd_send, upd_recv,
):
    order = pivot_ref.shape[1]
    own_rows = pivot_ref.shape[0]
    upd = coupling_ref.shape[0]
    blocks = order // BLK
    child = lax.axis_index("front")
    me = lax.axis_index("pair")
    sibling = lax.rem(child, SIBLINGS)
    sib_hi, sib_lo = lax.div(sibling, 2), lax.rem(sibling, 2)
    chip, core = lax.div(me, 2), lax.rem(me, 2)
    across = (1 - chip) * 2 + core
    mate = chip * 2 + (1 - core)
    mate_across = (1 - chip) * 2 + (1 - core)

    def relative(apart):
        hi = 1 - sib_hi if apart >= 2 else sib_hi
        lo = 1 - sib_lo if apart % 2 else sib_lo
        return hi * 2 + lo

    def sib_child(apart):
        return child - sibling + relative(apart)

    barrier = pltpu.get_barrier_semaphore()
    for peer in (across, mate):
        pl.semaphore_signal(barrier, inc=1, device_id={"pair": peer}, device_id_type=MESH)
    for apart in (1, 2, 3):
        pl.semaphore_signal(
            barrier, inc=1, device_id={"front": sib_child(apart)}, device_id_type=MESH
        )
    load_old = pltpu.make_async_copy(trailing_ref, old_flat, old_sem)
    load_old.start()
    pl.semaphore_wait(barrier, 5)

    def cols(k):
        return pl.ds(pl.multiple_of(k * BLK, BLK), BLK)

    def pivot_rows(owner):
        return pl.ds(pl.multiple_of(owner * own_rows, 8), own_rows)

    def pivot_copy(kind, k, owner, peer):
        spot = raw.at[pivot_rows(owner), cols(k)]
        return pltpu.make_async_remote_copy(
            src_ref=spot if kind == 2 else pivot_ref.at[:, cols(k)],
            dst_ref=spot,
            send_sem=piv_send.at[kind, k],
            recv_sem=piv_recv.at[kind, k],
            device_id={"pair": peer},
            device_id_type=MESH,
        )

    def panel_copy(kind, k, owner, peer):
        spot = panels.at[owner, :, cols(k)]
        return pltpu.make_async_remote_copy(
            src_ref=spot,
            dst_ref=spot,
            send_sem=pan_send.at[kind, k],
            recv_sem=pan_recv.at[kind, k],
            device_id={"pair": peer},
            device_id_type=MESH,
        )

    def relay(copy, k):
        copy(0, k, across, across).wait_recv()
        copy(2, k, across, mate).start()

    for k in range(blocks):
        pivot_copy(0, k, me, across).start()
        pivot_copy(1, k, me, mate).start()

    raw[pivot_rows(me), :] = pivot_ref[...]
    rows_left[...] = coupling_ref[...]
    work[...] = jnp.zeros_like(work)
    load_old.wait()
    for b in range(SIBLINGS):
        old[b] = old_flat[:, b * upd : (b + 1) * upd]
    relay(pivot_copy, 0)

    pend[...] = jnp.zeros_like(pend)
    pend_own[...] = jnp.zeros_like(pend_own)
    row_id = lax.broadcasted_iota(jnp.int32, (order, BLK), 0)

    def step(k, carry):
        at = cols(k)
        pivot_copy(1, k, mate, mate).wait_recv()
        pivot_copy(2, k, mate_across, mate).wait_recv()
        corner = (pend[0, at, :], pend[1, at, :])
        inverse = halves(inverse_factor(raw[at, at] + (work[at, at] - dot3(corner, corner))))
        last = (pend[0], pend[1])
        last_own = (pend_own[0], pend_own[1])
        for c in range(0, order, 256):
            cs = slice(c, c + 256)
            part = (last[0][cs], last[1][cs])
            work[:, cs] = work[:, cs] - dot3(last, part)
            rows_left[:, cs] = rows_left[:, cs] - dot3(last_own, part)

        @pl.when(k + 1 < blocks)
        def _():
            relay(pivot_copy, k + 1)

        @pl.when(k > 0)
        def _():
            relay(panel_copy, k - 1)

        solved = dot3(halves(rows_left[:, at]), inverse)
        factor_ref[:, at] = solved
        solved = halves(solved)
        panels[me, :, at] = solved[0]
        panel_copy(0, k, me, across).start()
        panel_copy(1, k, me, mate).start()
        column = jnp.where(row_id >= k * BLK, raw[:, at] + work[:, at], 0.0)
        panel = halves(dot3(halves(column), inverse))
        for half in range(2):
            pend[half] = panel[half]
            pend_own[half] = solved[half]
        return carry

    lax.fori_loop(0, blocks, step, 0)

    most = order - BLK

    def early(apart):
        there = relative(apart)
        old[there] = old[there] - dot_t(panels[me, :, :most], panels[there, :, :most])

    for k in range(blocks - 1):
        panel_copy(1, k, mate, mate).wait_recv()
        panel_copy(2, k, mate_across, mate).wait_recv()
    early(3)
    relay(panel_copy, blocks - 1)
    for apart in (1, 2, 0):
        early(apart)
    panel_copy(1, blocks - 1, mate, mate).wait_recv()
    panel_copy(2, blocks - 1, mate_across, mate).wait_recv()

    full = upd // BLK * BLK
    folds = BLK // (upd - full)
    fold_rows = upd // folds
    fold = [slice(f * fold_rows, (f + 1) * fold_rows) for f in range(folds)]

    def update_copies(apart):
        return [
            pltpu.make_async_remote_copy(
                src_ref=source.at[apart],
                dst_ref=target.at[apart - 1],
                send_sem=upd_send.at[which, apart],
                recv_sem=upd_recv.at[which, apart],
                device_id={"front": sib_child(apart)},
                device_id_type=MESH,
            )
            for which, (source, target) in enumerate(
                ((outgoing, incoming), (outgoing_tail, incoming_tail))
            )
        ]

    for apart in (3, 1, 2, 0):
        there = relative(apart)
        piece = old[there] - dot_t(panels[me, :, most:], panels[there, :, most:])
        outgoing[apart] = piece[:, :full].astype(jnp.bfloat16)
        outgoing_tail[apart] = jnp.concatenate([piece[f, full:] for f in fold], axis=1).astype(
            jnp.bfloat16
        )
        if apart:
            for copy in update_copies(apart):
                copy.start()

    row_count, col_count = front_ref.shape
    target_rows = lax.broadcasted_iota(jnp.int32, (row_count, upd), 0)
    target_cols = lax.broadcasted_iota(jnp.int32, (col_count, upd), 0)
    tail_lane = lax.broadcasted_iota(jnp.int32, (col_count, BLK), 1)

    def one_hot(targets, sources):
        return jnp.where(targets == sources, 1.0, 0.0).astype(jnp.bfloat16)

    def map_block(child_map, which):
        found = jnp.zeros((1, upd), jnp.int32)
        for b in range(SIBLINGS):
            found = jnp.where(which == b, child_map[:, b * upd : (b + 1) * upd], found)
        return found

    for apart in (0, 1, 2, 3):
        child_map = maps_ref[pl.ds(sib_child(apart), 1), :]
        rows_map = map_block(child_map, me) - me * row_count
        cols_map = map_block(child_map, sibling) - sibling * col_count
        tail_map = jnp.concatenate([cols_map[:, full:]] * folds, axis=1)
        row_hot = one_hot(target_rows, rows_map)
        col_hot = one_hot(target_cols[:, :full], cols_map[:, :full])
        tail_hot = [
            one_hot(
                jnp.where(lax.div(tail_lane, upd - full) == f, target_cols[:, :BLK], -1), tail_map
            )
            for f in range(folds)
        ]
        if apart:
            for copy in update_copies(apart):
                copy.wait_recv()
            value, tail = incoming[apart - 1], incoming_tail[apart - 1]
        else:
            value, tail = outgoing[0], outgoing_tail[0]
        moved = dot_t(value, col_hot) + jnp.concatenate(
            [dot_t(tail, hot) for hot in tail_hot], axis=0
        )
        placed = jnp.dot(row_hot, moved.astype(jnp.bfloat16), preferred_element_type=jnp.float32)
        if apart:
            front_ref[...] += placed
        else:
            front_ref[...] = placed

    for k in range(blocks):
        for kind, owner, peer in ((0, me, across), (1, me, mate), (2, across, mate)):
            pivot_copy(kind, k, owner, peer).wait_send()
            panel_copy(kind, k, owner, peer).wait_send()
    for apart in (1, 2, 3):
        for copy in update_copies(apart):
            copy.wait_send()


def body(pivot_block, coupling_rows, trailing_block, index_map):
    pairs = lax.axis_size("pair")
    own_rows, order = pivot_block.shape[1:]
    upd, upd_all = trailing_block.shape[1:]
    blocks = order // BLK
    row_count, col_count = PO // pairs, PO // SIBLINGS
    full = upd // BLK * BLK
    folded = upd * (upd - full) // BLK
    vmem = pl.BlockSpec(memory_space=pltpu.VMEM)
    factor, front = pl.pallas_call(
        fused_kernel,
        out_shape=(
            jax.ShapeDtypeStruct((upd, order), jnp.float32),
            jax.ShapeDtypeStruct((row_count, col_count), jnp.float32),
        ),
        in_specs=[vmem, vmem, vmem, pl.BlockSpec(memory_space=pl.ANY)],
        out_specs=[vmem, vmem],
        scratch_shapes=[
            pltpu.VMEM((order, order), jnp.float32),
            pltpu.VMEM((order, order), jnp.float32),
            pltpu.VMEM((upd, order), jnp.float32),
            pltpu.VMEM((pairs, upd, order), jnp.bfloat16),
            pltpu.VMEM((2, order, BLK), jnp.bfloat16),
            pltpu.VMEM((2, upd, BLK), jnp.bfloat16),
            pltpu.VMEM((upd, upd_all), jnp.float32),
            pltpu.VMEM((SIBLINGS, upd, upd), jnp.float32),
            pltpu.VMEM((SIBLINGS, upd, full), jnp.bfloat16),
            pltpu.VMEM((SIBLINGS, folded, BLK), jnp.bfloat16),
            pltpu.VMEM((SIBLINGS - 1, upd, full), jnp.bfloat16),
            pltpu.VMEM((SIBLINGS - 1, folded, BLK), jnp.bfloat16),
            pltpu.SemaphoreType.DMA,
            pltpu.SemaphoreType.DMA((3, blocks)),
            pltpu.SemaphoreType.DMA((3, blocks)),
            pltpu.SemaphoreType.DMA((3, blocks)),
            pltpu.SemaphoreType.DMA((3, blocks)),
            pltpu.SemaphoreType.DMA((2, SIBLINGS)),
            pltpu.SemaphoreType.DMA((2, SIBLINGS)),
        ],
        compiler_params=pltpu.CompilerParams(
            collective_id=0, has_side_effects=True, vmem_limit_bytes=56 * 2**20
        ),
    )(index_map, pivot_block[0], coupling_rows[0], trailing_block[0])
    return (factor[None, :, :], front[:, None, :])


def solution(mesh):
    in_specs = (P("front", "pair", None), P("front", "pair", None), P("front", "pair", None), P())
    out_specs = (P("front", "pair", None), P("pair", "front", None))
    return jax.shard_map(body, mesh=mesh, in_specs=in_specs, out_specs=out_specs, check_vma=False)
```

```python
import jax
import jax.numpy as jnp
from jax import lax
from jax.experimental import pallas as pl
from jax.experimental.pallas import tpu as pltpu
from jax.sharding import PartitionSpec as P

PO = 3072
SIBLINGS = 4
BLK = 128
SUB = 8
MESH = pl.DeviceIdType.MESH


def dot_t(a, b):
    return lax.dot_general(a, b, (((1,), (1,)), ((), ())), preferred_element_type=jnp.float32)


def halves(value):
    high = value.astype(jnp.bfloat16)
    return high, (value - high.astype(jnp.float32)).astype(jnp.bfloat16)


def dot3(a, b):
    return dot_t(
        jnp.concatenate([a[0], a[0], a[1]], axis=1), jnp.concatenate([b[0], b[1], b[0]], axis=1)
    )


def inverse_factor(block):
    size = block.shape[0]
    sub = lax.broadcasted_iota(jnp.int32, (SUB, size), 0)
    lane = lax.broadcasted_iota(jnp.int32, (SUB, size), 1)
    row_id = lax.broadcasted_iota(jnp.int32, (size, size), 0)
    col_id = lax.broadcasted_iota(jnp.int32, (size, size), 1)
    diagonal = jnp.where(row_id == col_id, block, 0.0)
    across = lax.rsqrt(jnp.sum(diagonal, axis=0, keepdims=True))
    down = lax.rsqrt(jnp.sum(diagonal, axis=1, keepdims=True))
    rest = block * across * down
    done = []
    for start in range(0, size, SUB):
        rows = size - start
        cols = [
            jnp.broadcast_to(rest[:, start + j : start + j + 1], (rows, size)) for j in range(SUB)
        ]
        rest_lane = lax.broadcasted_iota(jnp.int32, (rows, size), 1)
        rest = jnp.where((rest_lane >= start) & (rest_lane < start + SUB), 0.0, rest)
        slab = jnp.where(lane - start == sub, 1.0, rest[:SUB])
        top = [c[:SUB] for c in cols]
        more = rows > SUB
        if more:
            below = rest[SUB:]
            low = [c[SUB:] for c in cols]
        scale = jnp.ones((SUB, size), jnp.float32)
        for t in range(0, SUB, 2):
            first, second = top[t], top[t + 1]
            a, b, c = first[t : t + 1], second[t : t + 1], second[t + 1 : t + 2]
            det = a * c - b * b
            recip = 1.0 / det
            recip_a = 1.0 / a
            scale = jnp.where(sub == t, lax.rsqrt(a), scale)
            scale = jnp.where(sub == t + 1, lax.rsqrt(det * recip_a), scale)
            a, b, c = a * recip, b * recip, c * recip
            ratio = second[t : t + 1] * recip_a

            def pair_of(value):
                g, h = value[t : t + 1], value[t + 1 : t + 2]
                return c * g - b * h, a * h - b * g

            for j in range(t + 2, SUB):
                one, two = pair_of(top[j])
                top[j] = top[j] - (first * one + second * two)
                if more:
                    low[j] = low[j] - (low[t] * one + low[t + 1] * two)
            one, two = pair_of(slab)
            upper = slab[t : t + 1]
            later = sub > t + 1
            change = jnp.where(later, first, 0.0) * one + jnp.where(later, second, 0.0) * two
            slab = slab - jnp.where(sub == t + 1, ratio * upper, change)
            if more:
                below = below - (low[t] * one + low[t + 1] * two)
        done.append(slab * scale)
        if more:
            rest = below
    return jnp.where(col_id <= row_id, jnp.concatenate(done, axis=0) * across, 0.0)


def fused_kernel(
    maps_ref, pivot_ref, coupling_ref, trailing_ref, factor_ref, front_ref,
    raw, work, rows_left, panels, pend, pend_own, old_flat, old,
    outgoing, outgoing_tail, incoming, incoming_tail,
    old_sem, piv_send, piv_recv, pan_send, pan_recv, upd_send, upd_recv,
):
    order = pivot_ref.shape[1]
    own_rows = pivot_ref.shape[0]
    upd = coupling_ref.shape[0]
    blocks = order // BLK
    child = lax.axis_index("front")
    me = lax.axis_index("pair")
    sibling = lax.rem(child, SIBLINGS)
    sib_hi, sib_lo = lax.div(sibling, 2), lax.rem(sibling, 2)
    chip, core = lax.div(me, 2), lax.rem(me, 2)
    across = (1 - chip) * 2 + core
    mate = chip * 2 + (1 - core)
    mate_across = (1 - chip) * 2 + (1 - core)

    def relative(apart):
        hi = 1 - sib_hi if apart >= 2 else sib_hi
        lo = 1 - sib_lo if apart % 2 else sib_lo
        return hi * 2 + lo

    def sib_child(apart):
        return child - sibling + relative(apart)

    barrier = pltpu.get_barrier_semaphore()
    for peer in (across, mate):
        pl.semaphore_signal(barrier, inc=1, device_id={"pair": peer}, device_id_type=MESH)
    for apart in (1, 2, 3):
        pl.semaphore_signal(
            barrier, inc=1, device_id={"front": sib_child(apart)}, device_id_type=MESH
        )
    load_old = pltpu.make_async_copy(trailing_ref, old_flat, old_sem)
    load_old.start()
    pl.semaphore_wait(barrier, 5)

    def cols(k):
        return pl.ds(pl.multiple_of(k * BLK, BLK), BLK)

    def pivot_rows(owner):
        return pl.ds(pl.multiple_of(owner * own_rows, 8), own_rows)

    def pivot_copy(kind, k, owner, peer):
        spot = raw.at[pivot_rows(owner), cols(k)]
        return pltpu.make_async_remote_copy(
            src_ref=spot if kind == 2 else pivot_ref.at[:, cols(k)],
            dst_ref=spot,
            send_sem=piv_send.at[kind, k],
            recv_sem=piv_recv.at[kind, k],
            device_id={"pair": peer},
            device_id_type=MESH,
        )

    def panel_copy(kind, k, owner, peer):
        spot = panels.at[owner, :, cols(k)]
        return pltpu.make_async_remote_copy(
            src_ref=spot,
            dst_ref=spot,
            send_sem=pan_send.at[kind, k],
            recv_sem=pan_recv.at[kind, k],
            device_id={"pair": peer},
            device_id_type=MESH,
        )

    def relay(copy, k):
        copy(0, k, across, across).wait_recv()
        copy(2, k, across, mate).start()

    for k in range(blocks):
        pivot_copy(0, k, me, across).start()
        pivot_copy(1, k, me, mate).start()

    raw[pivot_rows(me), :] = pivot_ref[...]
    rows_left[...] = coupling_ref[...]
    work[...] = jnp.zeros_like(work)
    load_old.wait()
    for b in range(SIBLINGS):
        old[b] = old_flat[:, b * upd : (b + 1) * upd]
    relay(pivot_copy, 0)

    pend[...] = jnp.zeros_like(pend)
    pend_own[...] = jnp.zeros_like(pend_own)
    row_id = lax.broadcasted_iota(jnp.int32, (order, BLK), 0)

    def step(k, carry):
        at = cols(k)
        pivot_copy(1, k, mate, mate).wait_recv()
        pivot_copy(2, k, mate_across, mate).wait_recv()
        corner = (pend[0, at, :], pend[1, at, :])
        inverse = halves(inverse_factor(raw[at, at] + (work[at, at] - dot3(corner, corner))))
        last = (pend[0], pend[1])
        last_own = (pend_own[0], pend_own[1])
        for c in range(0, order, 256):
            cs = slice(c, c + 256)
            part = (last[0][cs], last[1][cs])
            work[:, cs] = work[:, cs] - dot3(last, part)
            rows_left[:, cs] = rows_left[:, cs] - dot3(last_own, part)

        @pl.when(k + 1 < blocks)
        def _():
            relay(pivot_copy, k + 1)

        @pl.when(k > 0)
        def _():
            relay(panel_copy, k - 1)

        solved = dot3(halves(rows_left[:, at]), inverse)
        factor_ref[:, at] = solved
        solved = halves(solved)
        panels[me, :, at] = solved[0]
        panel_copy(0, k, me, across).start()
        panel_copy(1, k, me, mate).start()
        column = jnp.where(row_id >= k * BLK, raw[:, at] + work[:, at], 0.0)
        panel = halves(dot3(halves(column), inverse))
        for half in range(2):
            pend[half] = panel[half]
            pend_own[half] = solved[half]
        return carry

    lax.fori_loop(0, blocks, step, 0)

    most = order - BLK

    def early(apart):
        there = relative(apart)
        old[there] = old[there] - dot_t(panels[me, :, :most], panels[there, :, :most])

    for k in range(blocks - 1):
        panel_copy(1, k, mate, mate).wait_recv()
        panel_copy(2, k, mate_across, mate).wait_recv()
    early(3)
    relay(panel_copy, blocks - 1)
    for apart in (1, 2, 0):
        early(apart)
    panel_copy(1, blocks - 1, mate, mate).wait_recv()
    panel_copy(2, blocks - 1, mate_across, mate).wait_recv()

    full = upd // BLK * BLK
    folds = BLK // (upd - full)
    fold_rows = upd // folds
    fold = [slice(f * fold_rows, (f + 1) * fold_rows) for f in range(folds)]

    def update_copies(apart):
        return [
            pltpu.make_async_remote_copy(
                src_ref=source.at[apart],
                dst_ref=target.at[apart - 1],
                send_sem=upd_send.at[which, apart],
                recv_sem=upd_recv.at[which, apart],
                device_id={"front": sib_child(apart)},
                device_id_type=MESH,
            )
            for which, (source, target) in enumerate(
                ((outgoing, incoming), (outgoing_tail, incoming_tail))
            )
        ]

    for apart in (3, 1, 2, 0):
        there = relative(apart)
        piece = old[there] - dot_t(panels[me, :, most:], panels[there, :, most:])
        outgoing[apart] = piece[:, :full].astype(jnp.bfloat16)
        outgoing_tail[apart] = jnp.concatenate([piece[f, full:] for f in fold], axis=1).astype(
            jnp.bfloat16
        )
        if apart:
            for copy in update_copies(apart):
                copy.start()

    row_count, col_count = front_ref.shape
    target_rows = lax.broadcasted_iota(jnp.int32, (row_count, upd), 0)
    target_cols = lax.broadcasted_iota(jnp.int32, (col_count, upd), 0)
    tail_lane = lax.broadcasted_iota(jnp.int32, (col_count, BLK), 1)

    def one_hot(targets, sources):
        return jnp.where(targets == sources, 1.0, 0.0).astype(jnp.bfloat16)

    def map_block(child_map, which):
        found = jnp.zeros((1, upd), jnp.int32)
        for b in range(SIBLINGS):
            found = jnp.where(which == b, child_map[:, b * upd : (b + 1) * upd], found)
        return found

    for apart in (0, 1, 2, 3):
        child_map = maps_ref[pl.ds(sib_child(apart), 1), :]
        rows_map = map_block(child_map, me) - me * row_count
        cols_map = map_block(child_map, sibling) - sibling * col_count
        tail_map = jnp.concatenate([cols_map[:, full:]] * folds, axis=1)
        row_hot = one_hot(target_rows, rows_map)
        col_hot = one_hot(target_cols[:, :full], cols_map[:, :full])
        tail_hot = [
            one_hot(
                jnp.where(lax.div(tail_lane, upd - full) == f, target_cols[:, :BLK], -1), tail_map
            )
            for f in range(folds)
        ]
        if apart:
            for copy in update_copies(apart):
                copy.wait_recv()
            value, tail = incoming[apart - 1], incoming_tail[apart - 1]
        else:
            value, tail = outgoing[0], outgoing_tail[0]
        moved = dot_t(value, col_hot) + jnp.concatenate(
            [dot_t(tail, hot) for hot in tail_hot], axis=0
        )
        placed = jnp.dot(row_hot, moved.astype(jnp.bfloat16), preferred_element_type=jnp.float32)
        if apart:
            front_ref[...] += placed
        else:
            front_ref[...] = placed

    for k in range(blocks):
        for kind, owner, peer in ((0, me, across), (1, me, mate), (2, across, mate)):
            pivot_copy(kind, k, owner, peer).wait_send()
            panel_copy(kind, k, owner, peer).wait_send()
    for apart in (1, 2, 3):
        for copy in update_copies(apart):
            copy.wait_send()


def body(pivot_block, coupling_rows, trailing_block, index_map):
    pairs = lax.axis_size("pair")
    own_rows, order = pivot_block.shape[1:]
    upd, upd_all = trailing_block.shape[1:]
    blocks = order // BLK
    row_count, col_count = PO // pairs, PO // SIBLINGS
    full = upd // BLK * BLK
    folded = upd * (upd - full) // BLK
    vmem = pl.BlockSpec(memory_space=pltpu.VMEM)
    factor, front = pl.pallas_call(
        fused_kernel,
        out_shape=(
            jax.ShapeDtypeStruct((upd, order), jnp.float32),
            jax.ShapeDtypeStruct((row_count, col_count), jnp.float32),
        ),
        in_specs=[vmem, vmem, vmem, pl.BlockSpec(memory_space=pl.ANY)],
        out_specs=[vmem, vmem],
        scratch_shapes=[
            pltpu.VMEM((order, order), jnp.float32),
            pltpu.VMEM((order, order), jnp.float32),
            pltpu.VMEM((upd, order), jnp.float32),
            pltpu.VMEM((pairs, upd, order), jnp.bfloat16),
            pltpu.VMEM((2, order, BLK), jnp.bfloat16),
            pltpu.VMEM((2, upd, BLK), jnp.bfloat16),
            pltpu.VMEM((upd, upd_all), jnp.float32),
            pltpu.VMEM((SIBLINGS, upd, upd), jnp.float32),
            pltpu.VMEM((SIBLINGS, upd, full), jnp.bfloat16),
            pltpu.VMEM((SIBLINGS, folded, BLK), jnp.bfloat16),
            pltpu.VMEM((SIBLINGS - 1, upd, full), jnp.bfloat16),
            pltpu.VMEM((SIBLINGS - 1, folded, BLK), jnp.bfloat16),
            pltpu.SemaphoreType.DMA,
            pltpu.SemaphoreType.DMA((3, blocks)),
            pltpu.SemaphoreType.DMA((3, blocks)),
            pltpu.SemaphoreType.DMA((3, blocks)),
            pltpu.SemaphoreType.DMA((3, blocks)),
            pltpu.SemaphoreType.DMA((2, SIBLINGS)),
            pltpu.SemaphoreType.DMA((2, SIBLINGS)),
        ],
        compiler_params=pltpu.CompilerParams(
            collective_id=0, has_side_effects=True, vmem_limit_bytes=56 * 2**20
        ),
    )(index_map, pivot_block[0], coupling_rows[0], trailing_block[0])
    return (factor[None, :, :], front[:, None, :])


def solution(mesh):
    in_specs = (P("front", "pair", None), P("front", "pair", None), P("front", "pair", None), P())
    out_specs = (P("front", "pair", None), P("pair", "front", None))
    return jax.shard_map(body, mesh=mesh, in_specs=in_specs, out_specs=out_specs, check_vma=False)
```

```python
import jax
import jax.numpy as jnp
from jax import lax
from jax.experimental import pallas as pl
from jax.experimental.pallas import tpu as pltpu
from jax.sharding import PartitionSpec as P

PO = 3072
SIBLINGS = 4
BLK = 128
SUB = 8
MESH = pl.DeviceIdType.MESH


def dot_t(a, b):
    return lax.dot_general(a, b, (((1,), (1,)), ((), ())), preferred_element_type=jnp.float32)


def halves(value):
    high = value.astype(jnp.bfloat16)
    return high, (value - high.astype(jnp.float32)).astype(jnp.bfloat16)


def dot3(a, b):
    return dot_t(
        jnp.concatenate([a[0], a[0], a[1]], axis=1), jnp.concatenate([b[0], b[1], b[0]], axis=1)
    )


def inverse_factor(block):
    size = block.shape[0]
    sub = lax.broadcasted_iota(jnp.int32, (SUB, size), 0)
    lane = lax.broadcasted_iota(jnp.int32, (SUB, size), 1)
    rest = block
    done = []
    for start in range(0, size, SUB):
        rows = size - start
        cols = [
            jnp.broadcast_to(rest[:, start + j : start + j + 1], (rows, size)) for j in range(SUB)
        ]
        rest_lane = lax.broadcasted_iota(jnp.int32, (rows, size), 1)
        rest = jnp.where((rest_lane >= start) & (rest_lane < start + SUB), 0.0, rest)
        slab = jnp.where(lane - start == sub, 1.0, rest[:SUB])
        top = [c[:SUB] for c in cols]
        more = rows > SUB
        if more:
            below = rest[SUB:]
            low = [c[SUB:] for c in cols]
        scale = jnp.ones((SUB, size), jnp.float32)
        for t in range(SUB):
            pivot = top[t][t : t + 1, :]
            recip = 1.0 / pivot
            scale = jnp.where(sub == t, lax.rsqrt(pivot), scale)
            for j in range(t + 1, SUB):
                mult = top[j][t : t + 1, :] * recip
                top[j] = top[j] - top[t] * mult
                if more:
                    low[j] = low[j] - low[t] * mult
            row = slab[t : t + 1, :] * recip
            slab = slab - jnp.where(sub > t, top[t], 0.0) * row
            if more:
                below = below - low[t] * row
        done.append(slab * scale)
        if more:
            rest = below
    whole = jnp.concatenate(done, axis=0)
    row_id = lax.broadcasted_iota(jnp.int32, (size, size), 0)
    col_id = lax.broadcasted_iota(jnp.int32, (size, size), 1)
    return jnp.where(col_id <= row_id, whole, 0.0)


def fused_kernel(
    maps_ref, pivot_ref, coupling_ref, trailing_ref, factor_out, front_ref,
    factor_ref, total, raw, work, rows_left, panels, pend, pend_own, old_flat, old,
    outgoing, outgoing_tail, incoming, incoming_tail,
    io_sem, piv_send, piv_recv, pan_send, pan_recv, upd_send, upd_recv,
):
    order = pivot_ref.shape[1]
    own_rows = pivot_ref.shape[0]
    upd = coupling_ref.shape[0]
    blocks = order // BLK
    child = lax.axis_index("front")
    me = lax.axis_index("pair")
    sibling = lax.rem(child, SIBLINGS)
    sib_hi, sib_lo = lax.div(sibling, 2), lax.rem(sibling, 2)
    chip, core = lax.div(me, 2), lax.rem(me, 2)
    across = (1 - chip) * 2 + core
    mate = chip * 2 + (1 - core)
    mate_across = (1 - chip) * 2 + (1 - core)

    def relative(apart):
        hi = 1 - sib_hi if apart >= 2 else sib_hi
        lo = 1 - sib_lo if apart % 2 else sib_lo
        return hi * 2 + lo

    def sib_child(apart):
        return child - sibling + relative(apart)

    barrier = pltpu.get_barrier_semaphore()
    for peer in (across, mate):
        pl.semaphore_signal(barrier, inc=1, device_id={"pair": peer}, device_id_type=MESH)
    for apart in (1, 2, 3):
        pl.semaphore_signal(
            barrier, inc=1, device_id={"front": sib_child(apart)}, device_id_type=MESH
        )
    load_rows = pltpu.make_async_copy(coupling_ref, rows_left, io_sem.at[0])
    load_rows.start()
    load_old = pltpu.make_async_copy(trailing_ref, old_flat, io_sem.at[1])
    load_old.start()
    pl.semaphore_wait(barrier, 5)

    def cols(k):
        return pl.ds(pl.multiple_of(k * BLK, BLK), BLK)

    def pivot_rows(owner):
        return pl.ds(pl.multiple_of(owner * own_rows, 8), own_rows)

    def pivot_copy(kind, k, owner, peer):
        spot = raw.at[pivot_rows(owner), cols(k)]
        return pltpu.make_async_remote_copy(
            src_ref=spot if kind == 2 else pivot_ref.at[:, cols(k)],
            dst_ref=spot,
            send_sem=piv_send.at[kind, k],
            recv_sem=piv_recv.at[kind, k],
            device_id={"pair": peer},
            device_id_type=MESH,
        )

    def panel_copy(kind, k, owner, peer):
        spot = panels.at[owner, :, cols(k)]
        return pltpu.make_async_remote_copy(
            src_ref=spot,
            dst_ref=spot,
            send_sem=pan_send.at[kind, k],
            recv_sem=pan_recv.at[kind, k],
            device_id={"pair": peer},
            device_id_type=MESH,
        )

    def relay(copy, k):
        copy(0, k, across, across).wait_recv()
        copy(2, k, across, mate).start()

    for k in range(blocks):
        pivot_copy(0, k, me, across).start()
        pivot_copy(1, k, me, mate).start()

    raw[pivot_rows(me), :] = pivot_ref[...]
    work[...] = jnp.zeros_like(work)
    load_rows.wait()
    load_old.wait()
    for b in range(SIBLINGS):
        old[b] = old_flat[:, b * upd : (b + 1) * upd]
    relay(pivot_copy, 0)

    pend[...] = jnp.zeros_like(pend)
    pend_own[...] = jnp.zeros_like(pend_own)
    row_id = lax.broadcasted_iota(jnp.int32, (order, BLK), 0)

    def step(k, carry):
        at = cols(k)
        pivot_copy(1, k, mate, mate).wait_recv()
        pivot_copy(2, k, mate_across, mate).wait_recv()
        corner = (pend[0, at, :], pend[1, at, :])
        inverse = halves(inverse_factor(raw[at, at] + (work[at, at] - dot3(corner, corner))))
        last = (pend[0], pend[1])
        last_own = (pend_own[0], pend_own[1])
        for c in range(0, order, 256):
            cs = slice(c, c + 256)
            part = (last[0][cs], last[1][cs])
            work[:, cs] = work[:, cs] - dot3(last, part)
            rows_left[:, cs] = rows_left[:, cs] - dot3(last_own, part)

        @pl.when(k + 1 < blocks)
        def _():
            relay(pivot_copy, k + 1)

        @pl.when(k == 2)
        def _():
            relay(panel_copy, 0)

        @pl.when(k >= 2)
        def _():
            relay(panel_copy, k - 1)

        solved = dot3(halves(rows_left[:, at]), inverse)
        factor_ref[:, at] = solved
        solved = halves(solved)
        panels[me, :, at] = solved[0]
        panel_copy(0, k, me, across).start()
        panel_copy(1, k, me, mate).start()
        column = jnp.where(row_id >= k * BLK, raw[:, at] + work[:, at], 0.0)
        panel = halves(dot3(halves(column), inverse))
        for half in range(2):
            pend[half] = panel[half]
            pend_own[half] = solved[half]
        return carry

    lax.fori_loop(0, blocks, step, 0)
    store_factor = pltpu.make_async_copy(factor_ref, factor_out, io_sem.at[2])
    store_factor.start()

    most = order - BLK

    def early(apart):
        there = relative(apart)
        old[there] = old[there] - dot_t(panels[me, :, :most], panels[there, :, :most])

    for k in range(blocks - 1):
        panel_copy(1, k, mate, mate).wait_recv()
        panel_copy(2, k, mate_across, mate).wait_recv()
    early(3)
    relay(panel_copy, blocks - 1)
    for apart in (1, 2, 0):
        early(apart)
    panel_copy(1, blocks - 1, mate, mate).wait_recv()
    panel_copy(2, blocks - 1, mate_across, mate).wait_recv()

    full = upd // BLK * BLK
    folds = BLK // (upd - full)
    fold_rows = upd // folds
    fold = [slice(f * fold_rows, (f + 1) * fold_rows) for f in range(folds)]

    def update_copies(apart):
        return [
            pltpu.make_async_remote_copy(
                src_ref=source.at[apart],
                dst_ref=target.at[apart - 1],
                send_sem=upd_send.at[which, apart],
                recv_sem=upd_recv.at[which, apart],
                device_id={"front": sib_child(apart)},
                device_id_type=MESH,
            )
            for which, (source, target) in enumerate(
                ((outgoing, incoming), (outgoing_tail, incoming_tail))
            )
        ]

    for apart in (3, 1, 2, 0):
        there = relative(apart)
        piece = old[there] - dot_t(panels[me, :, most:], panels[there, :, most:])
        outgoing[apart] = piece[:, :full].astype(jnp.bfloat16)
        outgoing_tail[apart] = jnp.concatenate([piece[f, full:] for f in fold], axis=1).astype(
            jnp.bfloat16
        )
        if apart:
            for copy in update_copies(apart):
                copy.start()

    row_count, col_count = total.shape
    target_rows = lax.broadcasted_iota(jnp.int32, (row_count, upd), 0)
    target_cols = lax.broadcasted_iota(jnp.int32, (col_count, upd), 0)
    tail_lane = lax.broadcasted_iota(jnp.int32, (col_count, BLK), 1)

    def one_hot(targets, sources):
        return jnp.where(targets == sources, 1.0, 0.0).astype(jnp.bfloat16)

    def map_block(child_map, which):
        found = jnp.zeros((1, upd), jnp.int32)
        for b in range(SIBLINGS):
            found = jnp.where(which == b, child_map[:, b * upd : (b + 1) * upd], found)
        return found

    for apart in (0, 1, 2, 3):
        child_map = maps_ref[pl.ds(sib_child(apart), 1), :]
        rows_map = map_block(child_map, me) - me * row_count
        cols_map = map_block(child_map, sibling) - sibling * col_count
        tail_map = jnp.concatenate([cols_map[:, full:]] * folds, axis=1)
        row_hot = one_hot(target_rows, rows_map)
        col_hot = one_hot(target_cols[:, :full], cols_map[:, :full])
        tail_hot = [
            one_hot(
                jnp.where(lax.div(tail_lane, upd - full) == f, target_cols[:, :BLK], -1), tail_map
            )
            for f in range(folds)
        ]
        if apart:
            for copy in update_copies(apart):
                copy.wait_recv()
            value, tail = incoming[apart - 1], incoming_tail[apart - 1]
        else:
            value, tail = outgoing[0], outgoing_tail[0]
        moved = dot_t(value, col_hot) + jnp.concatenate(
            [dot_t(tail, hot) for hot in tail_hot], axis=0
        )
        placed = jnp.dot(row_hot, moved.astype(jnp.bfloat16), preferred_element_type=jnp.float32)
        if apart == 0:
            total[...] = placed
        elif apart < SIBLINGS - 1:
            total[...] += placed
        else:
            front_ref[:, 0, :] = total[...] + placed

    for k in range(blocks):
        for kind, owner, peer in ((0, me, across), (1, me, mate), (2, across, mate)):
            pivot_copy(kind, k, owner, peer).wait_send()
            panel_copy(kind, k, owner, peer).wait_send()
    for apart in (1, 2, 3):
        for copy in update_copies(apart):
            copy.wait_send()
    store_factor.wait()


def body(pivot_block, coupling_rows, trailing_block, index_map):
    pairs = lax.axis_size("pair")
    own_rows, order = pivot_block.shape[1:]
    upd, upd_all = trailing_block.shape[1:]
    blocks = order // BLK
    row_count, col_count = PO // pairs, PO // SIBLINGS
    full = upd // BLK * BLK
    folded = upd * (upd - full) // BLK
    vmem = pl.BlockSpec(memory_space=pltpu.VMEM)
    hbm = pl.BlockSpec(memory_space=pl.ANY)
    factor, front = pl.pallas_call(
        fused_kernel,
        out_shape=(
            jax.ShapeDtypeStruct((upd, order), jnp.float32),
            jax.ShapeDtypeStruct((row_count, 1, col_count), jnp.float32),
        ),
        in_specs=[vmem, vmem, hbm, hbm],
        out_specs=[hbm, vmem],
        scratch_shapes=[
            pltpu.VMEM((upd, order), jnp.float32),
            pltpu.VMEM((row_count, col_count), jnp.float32),
            pltpu.VMEM((order, order), jnp.float32),
            pltpu.VMEM((order, order), jnp.float32),
            pltpu.VMEM((upd, order), jnp.float32),
            pltpu.VMEM((pairs, upd, order), jnp.bfloat16),
            pltpu.VMEM((2, order, BLK), jnp.bfloat16),
            pltpu.VMEM((2, upd, BLK), jnp.bfloat16),
            pltpu.VMEM((upd, upd_all), jnp.float32),
            pltpu.VMEM((SIBLINGS, upd, upd), jnp.float32),
            pltpu.VMEM((SIBLINGS, upd, full), jnp.bfloat16),
            pltpu.VMEM((SIBLINGS, folded, BLK), jnp.bfloat16),
            pltpu.VMEM((SIBLINGS - 1, upd, full), jnp.bfloat16),
            pltpu.VMEM((SIBLINGS - 1, folded, BLK), jnp.bfloat16),
            pltpu.SemaphoreType.DMA((3,)),
            pltpu.SemaphoreType.DMA((3, blocks)),
            pltpu.SemaphoreType.DMA((3, blocks)),
            pltpu.SemaphoreType.DMA((3, blocks)),
            pltpu.SemaphoreType.DMA((3, blocks)),
            pltpu.SemaphoreType.DMA((2, SIBLINGS)),
            pltpu.SemaphoreType.DMA((2, SIBLINGS)),
        ],
        compiler_params=pltpu.CompilerParams(
            collective_id=0, has_side_effects=True, vmem_limit_bytes=56 * 2**20
        ),
    )(index_map, pivot_block[0], coupling_rows[0], trailing_block[0])
    return (factor[None, :, :], front)


def solution(mesh):
    in_specs = (P("front", "pair", None), P("front", "pair", None), P("front", "pair", None), P())
    out_specs = (P("front", "pair", None), P("pair", "front", None))
    return jax.shard_map(body, mesh=mesh, in_specs=in_specs, out_specs=out_specs, check_vma=False)
```

```python
import jax
import jax.numpy as jnp
from jax import lax
from jax.experimental import pallas as pl
from jax.experimental.pallas import tpu as pltpu
from jax.sharding import PartitionSpec as P

PO = 3072
SIBLINGS = 4
BLK = 128
SUB = 8
MESH = pl.DeviceIdType.MESH


def dot_t(a, b):
    return lax.dot_general(a, b, (((1,), (1,)), ((), ())), preferred_element_type=jnp.float32)


def halves(value):
    high = value.astype(jnp.bfloat16)
    return high, (value - high.astype(jnp.float32)).astype(jnp.bfloat16)


def dot3(a, b):
    return dot_t(
        jnp.concatenate([a[0], a[0], a[1]], axis=1), jnp.concatenate([b[0], b[1], b[0]], axis=1)
    )


def inverse_factor(block):
    size = block.shape[0]
    sub = lax.broadcasted_iota(jnp.int32, (SUB, size), 0)
    lane = lax.broadcasted_iota(jnp.int32, (SUB, size), 1)
    rest = block
    done = []
    for start in range(0, size, SUB):
        rows = size - start
        cols = [
            jnp.broadcast_to(rest[:, start + j : start + j + 1], (rows, size)) for j in range(SUB)
        ]
        rest_lane = lax.broadcasted_iota(jnp.int32, (rows, size), 1)
        rest = jnp.where((rest_lane >= start) & (rest_lane < start + SUB), 0.0, rest)
        slab = jnp.where(lane - start == sub, 1.0, rest[:SUB])
        top = [c[:SUB] for c in cols]
        more = rows > SUB
        if more:
            below = rest[SUB:]
            low = [c[SUB:] for c in cols]
        scale = jnp.ones((SUB, size), jnp.float32)
        for t in range(SUB):
            pivot = top[t][t : t + 1, :]
            recip = 1.0 / pivot
            scale = jnp.where(sub == t, lax.rsqrt(pivot), scale)
            for j in range(t + 1, SUB):
                mult = top[j][t : t + 1, :] * recip
                top[j] = top[j] - top[t] * mult
                if more:
                    low[j] = low[j] - low[t] * mult
            row = slab[t : t + 1, :] * recip
            slab = slab - jnp.where(sub > t, top[t], 0.0) * row
            if more:
                below = below - low[t] * row
        done.append(slab * scale)
        if more:
            rest = below
    whole = jnp.concatenate(done, axis=0)
    row_id = lax.broadcasted_iota(jnp.int32, (size, size), 0)
    col_id = lax.broadcasted_iota(jnp.int32, (size, size), 1)
    return jnp.where(col_id <= row_id, whole, 0.0)


def fused_kernel(
    maps_ref, pivot_ref, coupling_ref, trailing_ref, factor_out, front_ref,
    factor_ref, total, raw, work, rows_left, panels, pend, pend_own, old_flat, old,
    outgoing, outgoing_tail, incoming, incoming_tail,
    io_sem, piv_send, piv_recv, pan_send, pan_recv, upd_send, upd_recv,
):
    order = pivot_ref.shape[1]
    own_rows = pivot_ref.shape[0]
    upd = coupling_ref.shape[0]
    blocks = order // BLK
    child = lax.axis_index("front")
    me = lax.axis_index("pair")
    sibling = lax.rem(child, SIBLINGS)
    sib_hi, sib_lo = lax.div(sibling, 2), lax.rem(sibling, 2)
    chip, core = lax.div(me, 2), lax.rem(me, 2)
    across = (1 - chip) * 2 + core
    mate = chip * 2 + (1 - core)
    mate_across = (1 - chip) * 2 + (1 - core)

    def relative(apart):
        hi = 1 - sib_hi if apart >= 2 else sib_hi
        lo = 1 - sib_lo if apart % 2 else sib_lo
        return hi * 2 + lo

    def sib_child(apart):
        return child - sibling + relative(apart)

    barrier = pltpu.get_barrier_semaphore()
    for peer in (across, mate):
        pl.semaphore_signal(barrier, inc=1, device_id={"pair": peer}, device_id_type=MESH)
    for apart in (1, 2, 3):
        pl.semaphore_signal(
            barrier, inc=1, device_id={"front": sib_child(apart)}, device_id_type=MESH
        )
    load_rows = pltpu.make_async_copy(coupling_ref, rows_left, io_sem.at[0])
    load_rows.start()
    load_old = pltpu.make_async_copy(trailing_ref, old_flat, io_sem.at[1])
    load_old.start()
    pl.semaphore_wait(barrier, 5)

    def cols(k):
        return pl.ds(pl.multiple_of(k * BLK, BLK), BLK)

    def pivot_rows(owner):
        return pl.ds(pl.multiple_of(owner * own_rows, 8), own_rows)

    def pivot_copy(kind, k, owner, peer):
        spot = raw.at[pivot_rows(owner), cols(k)]
        return pltpu.make_async_remote_copy(
            src_ref=spot if kind == 2 else pivot_ref.at[:, cols(k)],
            dst_ref=spot,
            send_sem=piv_send.at[kind, k],
            recv_sem=piv_recv.at[kind, k],
            device_id={"pair": peer},
            device_id_type=MESH,
        )

    def panel_copy(kind, k, owner, peer):
        spot = panels.at[owner, :, cols(k)]
        return pltpu.make_async_remote_copy(
            src_ref=spot,
            dst_ref=spot,
            send_sem=pan_send.at[kind, k],
            recv_sem=pan_recv.at[kind, k],
            device_id={"pair": peer},
            device_id_type=MESH,
        )

    def relay(copy, k):
        copy(0, k, across, across).wait_recv()
        copy(2, k, across, mate).start()

    for k in range(blocks):
        pivot_copy(0, k, me, across).start()
        pivot_copy(1, k, me, mate).start()

    raw[pivot_rows(me), :] = pivot_ref[...]
    work[...] = jnp.zeros_like(work)
    load_rows.wait()
    load_old.wait()
    for b in range(SIBLINGS):
        old[b] = old_flat[:, b * upd : (b + 1) * upd]
    relay(pivot_copy, 0)

    pend[...] = jnp.zeros_like(pend)
    pend_own[...] = jnp.zeros_like(pend_own)
    row_id = lax.broadcasted_iota(jnp.int32, (order, BLK), 0)

    def step(k, carry):
        at = cols(k)
        pivot_copy(1, k, mate, mate).wait_recv()
        pivot_copy(2, k, mate_across, mate).wait_recv()
        corner = (pend[0, at, :], pend[1, at, :])
        inverse = halves(inverse_factor(raw[at, at] + (work[at, at] - dot3(corner, corner))))
        last = (pend[0], pend[1])
        last_own = (pend_own[0], pend_own[1])
        for c in range(0, order, 256):
            cs = slice(c, c + 256)
            part = (last[0][cs], last[1][cs])
            work[:, cs] = work[:, cs] - dot3(last, part)
            rows_left[:, cs] = rows_left[:, cs] - dot3(last_own, part)

        @pl.when(k + 1 < blocks)
        def _():
            relay(pivot_copy, k + 1)

        @pl.when(k == 2)
        def _():
            relay(panel_copy, 0)

        @pl.when(k >= 2)
        def _():
            relay(panel_copy, k - 1)

        solved = dot3(halves(rows_left[:, at]), inverse)
        factor_ref[:, at] = solved
        solved = halves(solved)
        panels[me, :, at] = solved[0]
        panel_copy(0, k, me, across).start()
        panel_copy(1, k, me, mate).start()
        column = jnp.where(row_id >= k * BLK, raw[:, at] + work[:, at], 0.0)
        panel = halves(dot3(halves(column), inverse))
        for half in range(2):
            pend[half] = panel[half]
            pend_own[half] = solved[half]
        return carry

    lax.fori_loop(0, blocks, step, 0)
    store_factor = pltpu.make_async_copy(factor_ref, factor_out, io_sem.at[2])
    store_factor.start()

    most = order - BLK

    def early(apart):
        there = relative(apart)
        old[there] = old[there] - dot_t(panels[me, :, :most], panels[there, :, :most])

    for k in range(blocks - 1):
        panel_copy(1, k, mate, mate).wait_recv()
        panel_copy(2, k, mate_across, mate).wait_recv()
    early(3)
    relay(panel_copy, blocks - 1)
    for apart in (1, 2, 0):
        early(apart)
    panel_copy(1, blocks - 1, mate, mate).wait_recv()
    panel_copy(2, blocks - 1, mate_across, mate).wait_recv()

    full = upd // BLK * BLK
    folds = BLK // (upd - full)
    fold_rows = upd // folds
    fold = [slice(f * fold_rows, (f + 1) * fold_rows) for f in range(folds)]

    def update_copies(apart):
        return [
            pltpu.make_async_remote_copy(
                src_ref=source.at[apart],
                dst_ref=target.at[apart - 1],
                send_sem=upd_send.at[which, apart],
                recv_sem=upd_recv.at[which, apart],
                device_id={"front": sib_child(apart)},
                device_id_type=MESH,
            )
            for which, (source, target) in enumerate(
                ((outgoing, incoming), (outgoing_tail, incoming_tail))
            )
        ]

    for apart in (3, 1, 2, 0):
        there = relative(apart)
        piece = old[there] - dot_t(panels[me, :, most:], panels[there, :, most:])
        outgoing[apart] = piece[:, :full].astype(jnp.bfloat16)
        outgoing_tail[apart] = jnp.concatenate([piece[f, full:] for f in fold], axis=1).astype(
            jnp.bfloat16
        )
        if apart:
            for copy in update_copies(apart):
                copy.start()

    row_count, col_count = total.shape
    target_rows = lax.broadcasted_iota(jnp.int32, (row_count, upd), 0)
    target_cols = lax.broadcasted_iota(jnp.int32, (col_count, upd), 0)
    tail_lane = lax.broadcasted_iota(jnp.int32, (col_count, BLK), 1)

    def one_hot(targets, sources):
        return jnp.where(targets == sources, 1.0, 0.0).astype(jnp.bfloat16)

    def map_block(child_map, which):
        found = jnp.zeros((1, upd), jnp.int32)
        for b in range(SIBLINGS):
            found = jnp.where(which == b, child_map[:, b * upd : (b + 1) * upd], found)
        return found

    for apart in (0, 3, 1, 2):
        child_map = maps_ref[pl.ds(sib_child(apart), 1), :]
        rows_map = map_block(child_map, me) - me * row_count
        cols_map = map_block(child_map, sibling) - sibling * col_count
        tail_map = jnp.concatenate([cols_map[:, full:]] * folds, axis=1)
        row_hot = one_hot(target_rows, rows_map)
        col_hot = one_hot(target_cols[:, :full], cols_map[:, :full])
        tail_hot = [
            one_hot(
                jnp.where(lax.div(tail_lane, upd - full) == f, target_cols[:, :BLK], -1), tail_map
            )
            for f in range(folds)
        ]
        if apart:
            for copy in update_copies(apart):
                copy.wait_recv()
            value, tail = incoming[apart - 1], incoming_tail[apart - 1]
        else:
            value, tail = outgoing[0], outgoing_tail[0]
        moved = dot_t(value, col_hot) + jnp.concatenate(
            [dot_t(tail, hot) for hot in tail_hot], axis=0
        )
        placed = jnp.dot(row_hot, moved.astype(jnp.bfloat16), preferred_element_type=jnp.float32)
        if apart == 0:
            total[...] = placed
        elif apart != 2:
            total[...] += placed
        else:
            front_ref[:, 0, :] = total[...] + placed

    for k in range(blocks):
        for kind, owner, peer in ((0, me, across), (1, me, mate), (2, across, mate)):
            pivot_copy(kind, k, owner, peer).wait_send()
            panel_copy(kind, k, owner, peer).wait_send()
    for apart in (1, 2, 3):
        for copy in update_copies(apart):
            copy.wait_send()
    store_factor.wait()


def body(pivot_block, coupling_rows, trailing_block, index_map):
    pairs = lax.axis_size("pair")
    own_rows, order = pivot_block.shape[1:]
    upd, upd_all = trailing_block.shape[1:]
    blocks = order // BLK
    row_count, col_count = PO // pairs, PO // SIBLINGS
    full = upd // BLK * BLK
    folded = upd * (upd - full) // BLK
    vmem = pl.BlockSpec(memory_space=pltpu.VMEM)
    hbm = pl.BlockSpec(memory_space=pl.ANY)
    factor, front = pl.pallas_call(
        fused_kernel,
        out_shape=(
            jax.ShapeDtypeStruct((upd, order), jnp.float32),
            jax.ShapeDtypeStruct((row_count, 1, col_count), jnp.float32),
        ),
        in_specs=[vmem, vmem, hbm, hbm],
        out_specs=[hbm, vmem],
        scratch_shapes=[
            pltpu.VMEM((upd, order), jnp.float32),
            pltpu.VMEM((row_count, col_count), jnp.float32),
            pltpu.VMEM((order, order), jnp.float32),
            pltpu.VMEM((order, order), jnp.float32),
            pltpu.VMEM((upd, order), jnp.float32),
            pltpu.VMEM((pairs, upd, order), jnp.bfloat16),
            pltpu.VMEM((2, order, BLK), jnp.bfloat16),
            pltpu.VMEM((2, upd, BLK), jnp.bfloat16),
            pltpu.VMEM((upd, upd_all), jnp.float32),
            pltpu.VMEM((SIBLINGS, upd, upd), jnp.float32),
            pltpu.VMEM((SIBLINGS, upd, full), jnp.bfloat16),
            pltpu.VMEM((SIBLINGS, folded, BLK), jnp.bfloat16),
            pltpu.VMEM((SIBLINGS - 1, upd, full), jnp.bfloat16),
            pltpu.VMEM((SIBLINGS - 1, folded, BLK), jnp.bfloat16),
            pltpu.SemaphoreType.DMA((3,)),
            pltpu.SemaphoreType.DMA((3, blocks)),
            pltpu.SemaphoreType.DMA((3, blocks)),
            pltpu.SemaphoreType.DMA((3, blocks)),
            pltpu.SemaphoreType.DMA((3, blocks)),
            pltpu.SemaphoreType.DMA((2, SIBLINGS)),
            pltpu.SemaphoreType.DMA((2, SIBLINGS)),
        ],
        compiler_params=pltpu.CompilerParams(
            collective_id=0, has_side_effects=True, vmem_limit_bytes=56 * 2**20
        ),
    )(index_map, pivot_block[0], coupling_rows[0], trailing_block[0])
    return (factor[None, :, :], front)


def solution(mesh):
    in_specs = (P("front", "pair", None), P("front", "pair", None), P("front", "pair", None), P())
    out_specs = (P("front", "pair", None), P("pair", "front", None))
    return jax.shard_map(body, mesh=mesh, in_specs=in_specs, out_specs=out_specs, check_vma=False)
```
